32 devices in a mesh: ctx: 16 (over z, y, x), tp: 2 (over core).
Axes of the slice: x: 2, y: 2, z: 4, core: 2. Of those that a mesh axis runs over, the one named last changes fastest.
Arguments:
- query_states: bfloat16 [8192, 4096], P('ctx', 'tp'), may hold values from -32 to 32
- rotated_key_states: bfloat16 [8192, 2048], P('ctx', 'tp'), may hold values from -32 to 32
- value_state_rows: bfloat16 [8192, 2048], P('ctx', 'tp'), may hold values from -6 to 6
- doc_ids: int32 [8192], P('ctx'), may hold values from 0 to 7, never falling along the last dimension, each value on 1 to 2048 neighbouring positions
- w_out: bfloat16 [4096, 5376], P('ctx', 'tp'), may hold values from -0.125 to 0.125
Outputs:
- mixed: bfloat16 [8192, 5376], P('ctx', 'tp')
The draws below stay inside these ranges and needn't reach their ends.
Inputs may be any that keep to these rules, and one draw needn't show every extreme that they name: `doc_ids`: document numbers never fall along the tokens; each document has 1 to 2048 tokens and one has exactly 2048.
All inputs are finite; a program needn't handle non-finite values.
Results may differ from the reference program's by a relative error of at most 0.0054.
Values may be sent and summed in bfloat16 or wider, within the bound.
A program may use at most 128 MiB of HBM per device.

```python
import math
import jax
import jax.numpy as jnp
import numpy as np
from jax import lax

D = 5376
QUERY_HEAD_COUNT = 32
KEY_VALUE_HEADS = 16
HEAD_SIZE = 128
LOOKBACK_SPAN = 1024
PACKED_TOKENS = 8192
DOCS = 8
MOST = 2048


def draw_shared(key):
    random_key_split = jax.random.fold_in(key, 101)
    key_query = jax.random.fold_in(key, 102)
    key_matrix = jax.random.truncated_normal(random_key_split, -4.0, 4.0, (PACKED_TOKENS, KEY_VALUE_HEADS, HEAD_SIZE), jnp.float32)
    query_matrix = jax.random.truncated_normal(key_query, -4.0, 4.0, (PACKED_TOKENS, QUERY_HEAD_COUNT, HEAD_SIZE), jnp.float32)
    key_matrix = jnp.clip(key_matrix, -32.0, 32.0).reshape(PACKED_TOKENS, KEY_VALUE_HEADS * HEAD_SIZE)
    query_matrix = jnp.clip(query_matrix, -32.0, 32.0).reshape(PACKED_TOKENS, QUERY_HEAD_COUNT * HEAD_SIZE)
    return (query_matrix, key_matrix)


def draw_query_states(key, part):
    return draw_shared(key)[0].astype(jnp.bfloat16)


def draw_rotated_key_states(key, part):
    return draw_shared(key)[1].astype(jnp.bfloat16)


def strengthened(entries, own_key, source, target, shards_of, factor):
    def block_of(position):
        return (jnp.arange(entries.shape[position]) // (entries.shape[position] // shards_of)).reshape((-1,) + (1,) * (entries.ndim - 1 - position))

    first = jax.random.permutation(own_key, shards_of)[block_of(target)]
    far = (block_of(target) + shards_of // 2) % shards_of
    return jnp.where((block_of(source) == first) | (block_of(source) == far), factor * entries, entries)


def shard_levels(rng, extent, split, low, largest):
    def one(dim, shards_of):
        draws = jax.random.uniform(jax.random.fold_in(jax.random.fold_in(rng, 6), dim), (shards_of,), jnp.float32, low / len(split), largest / len(split))
        return jnp.repeat(jnp.exp(draws), extent[dim] // shards_of).reshape((-1,) + (1,) * (len(extent) - dim - 1))

    loudness = one(*split[0])
    for cut in split[1:]:
        loudness = loudness * one(*cut)
    return loudness


def length_profile(amount, total, bound, lean):
    loads = [(1 << 20) // math.isqrt(standing ** lean) + 1 for standing in range(2, amount + 1)]
    spare, counts = total - bound - (amount - 1), [1] * (amount - 1)
    while spare > 0:
        candidates = [i for i in range(amount - 1) if counts[i] < bound]
        mass, budget = sum([loads[i] for i in candidates]), spare
        for i in candidates:
            extra = min(bound - counts[i], max(1, budget * loads[i] // mass), spare)
            counts[i] = counts[i] + extra
            spare = spare - extra
    return np.array([bound] + counts)


def ragged_sizes(stream_key, amount, total, limit, lean):
    if amount == 2:
        one = jax.random.randint(stream_key, (), max(1, total - limit), min(limit, total - 1) + 1)
        return jnp.stack([one, total - one])
    sizes = jnp.asarray(length_profile(amount, total, limit, lean), jnp.int32)
    pairs = (amount - 1) // 2
    source_of, taker = sizes[1:1 + 2 * pairs:2], sizes[2:2 + 2 * pairs:2]
    margin = jnp.minimum(source_of - 1, limit - taker)
    shifted = jax.random.randint(jax.random.fold_in(stream_key, 1), (pairs,), 0, 1 << 20) % (margin + 1)
    sizes = sizes.at[1:1 + 2 * pairs:2].set(source_of - shifted).at[2:2 + 2 * pairs:2].set(taker + shifted)
    return sizes[jax.random.permutation(jax.random.fold_in(stream_key, 2), amount)]


def noise(own_key, dims, deviation, limit, pieces=(), kind=jnp.bfloat16):
    values = deviation * jax.random.normal(own_key, dims, jnp.float32)
    if pieces:
        values = values * shard_levels(own_key, dims, pieces, -0.22, 0.18)
    return jnp.clip(values, -limit, limit).astype(kind)


def noise_with(key, shape, deviation, reach, shards, heavy, held_as=jnp.bfloat16):
    entries = deviation * jax.random.normal(key, shape, jnp.float32)
    if shards:
        entries = entries * shard_levels(key, shape, shards, -0.22, 0.18)
    return jnp.clip(strengthened(entries, jax.random.fold_in(key, 3), *heavy), -reach, reach).astype(held_as)


def setup_inputs(seed: int = 0) -> dict:
    arg_keys = jax.random.split(jax.random.key(seed), 6)
    return {
        "query_states": draw_query_states(jax.random.fold_in(arg_keys[5], 71), 0),
        "rotated_key_states": draw_rotated_key_states(jax.random.fold_in(arg_keys[5], 71), 0),
        "value_state_rows": noise(arg_keys[2], (PACKED_TOKENS, KEY_VALUE_HEADS * HEAD_SIZE), 1.0, 6.0, ((0, 16), (1, 2))),
        "doc_ids": jnp.searchsorted(jnp.cumsum(ragged_sizes(arg_keys[3], DOCS, PACKED_TOKENS, MOST, 2)), jnp.arange(PACKED_TOKENS), side="right").astype(jnp.int32),
        "w_out": noise_with(arg_keys[4], (QUERY_HEAD_COUNT * HEAD_SIZE, D), (QUERY_HEAD_COUNT * HEAD_SIZE) ** -0.5, 0.125, ((0, 16), (1, 2)), (0, 1, 16, 2.0)),
    }


attn_scale = 168.0 ** -0.5


def attend(query_states, rotated_key_states, value_state_rows, doc_ids):
    queries_per_group = QUERY_HEAD_COUNT // KEY_VALUE_HEADS
    block_total = PACKED_TOKENS // LOOKBACK_SPAN
    padded_keys = jnp.concatenate([jnp.zeros((LOOKBACK_SPAN, KEY_VALUE_HEADS * HEAD_SIZE), rotated_key_states.dtype), rotated_key_states], 0)
    padded_values = jnp.concatenate([jnp.zeros((LOOKBACK_SPAN, KEY_VALUE_HEADS * HEAD_SIZE), value_state_rows.dtype), value_state_rows], 0)
    docs_pad = jnp.concatenate([jnp.full((LOOKBACK_SPAN,), -1, jnp.int32), doc_ids.astype(jnp.int32)], 0)

    def one_block(block_id):
        offset = (block_id * LOOKBACK_SPAN).astype(jnp.int32)
        query_row_block = lax.dynamic_slice_in_dim(query_states, offset, LOOKBACK_SPAN, 0).astype(jnp.float32)
        query_row_block = query_row_block.reshape(LOOKBACK_SPAN, KEY_VALUE_HEADS, queries_per_group, HEAD_SIZE)
        key_row_block = lax.dynamic_slice_in_dim(padded_keys, offset, 2 * LOOKBACK_SPAN, 0).astype(jnp.float32)
        key_row_block = key_row_block.reshape(2 * LOOKBACK_SPAN, KEY_VALUE_HEADS, HEAD_SIZE)
        value_row_block = lax.dynamic_slice_in_dim(padded_values, offset, 2 * LOOKBACK_SPAN, 0).astype(jnp.float32)
        value_row_block = value_row_block.reshape(2 * LOOKBACK_SPAN, KEY_VALUE_HEADS, HEAD_SIZE)
        query_docs = lax.dynamic_slice_in_dim(doc_ids.astype(jnp.int32), offset, LOOKBACK_SPAN, 0)
        key_docs = lax.dynamic_slice_in_dim(docs_pad, offset, 2 * LOOKBACK_SPAN, 0)
        query_pos = jnp.arange(LOOKBACK_SPAN, dtype=jnp.int32) + LOOKBACK_SPAN
        key_pos = jnp.arange(2 * LOOKBACK_SPAN, dtype=jnp.int32)
        distance = query_pos[:, None] - key_pos[None, :]
        visible = (query_docs[:, None] == key_docs[None, :]) & (distance >= 0) & (distance < LOOKBACK_SPAN)
        scores = jnp.einsum("qhgd,khd->hgqk", query_row_block, key_row_block) * attn_scale
        scores = jnp.where(visible, scores, -jnp.inf)
        row_max = jnp.max(scores, axis=3, keepdims=True)
        weights = jnp.exp(scores - row_max)
        weight_sum = jnp.sum(weights, axis=3)
        rounded = lax.optimization_barrier(weights.astype(jnp.bfloat16)).astype(jnp.float32)
        numer = jnp.einsum("hgqk,khd->qhgd", rounded, value_row_block)
        result = numer / jnp.transpose(weight_sum, (2, 0, 1))[..., None]
        return result.astype(jnp.bfloat16).reshape(LOOKBACK_SPAN, QUERY_HEAD_COUNT * HEAD_SIZE)

    blocks = lax.map(one_block, jnp.arange(block_total, dtype=jnp.int32))
    return blocks.reshape(PACKED_TOKENS, QUERY_HEAD_COUNT * HEAD_SIZE)


def reference(query_states, rotated_key_states, value_state_rows, doc_ids, w_out):
    attended = attend(query_states, rotated_key_states, value_state_rows, doc_ids)
    summed = jnp.dot(attended, w_out, preferred_element_type=jnp.float32)
    return summed.astype(jnp.bfloat16)
```

```python
import functools
import jax
import jax.numpy as jnp
from jax import lax
from jax.experimental import pallas as pl
from jax.experimental.pallas import tpu as pltpu
from jax.sharding import PartitionSpec as P

HEAD_SIZE = 128
LOOKBACK_SPAN = 1024
HIDDEN = -1e30

attn_scale = 168.0 ** (-0.5)
exp2_scale = attn_scale * 1.4426950408889634


def shifted(value, axis, by):
    peers = lax.axis_size(axis)
    pairs = [(i, i + by) for i in range(peers) if 0 <= i + by < peers]
    return lax.ppermute(value, axis, pairs)


def swapped(value, axis):
    return lax.ppermute(value, axis, [(i, i ^ 1) for i in range(lax.axis_size(axis))])


def attend_kernel(blocks, group, tile, *refs):
    q_ref = refs[1]
    k_refs = refs[2 : 2 + blocks]
    v_refs = refs[2 + blocks : 2 + 2 * blocks]
    qdoc_ref, kdoc_ref, o_ref, bias = refs[2 + 2 * blocks :]
    rows = q_ref.shape[0]
    span = LOOKBACK_SPAN + tile

    @pl.when(pl.program_id(0) == 0)
    def _():
        for t in range(rows // tile):
            near = t * tile
            col = lax.broadcasted_iota(jnp.int32, (tile, span), 1)
            row = lax.broadcasted_iota(jnp.int32, (tile, span), 0)
            ahead = row + LOOKBACK_SPAN - col
            same = qdoc_ref[near : near + tile, :] == kdoc_ref[:, near : near + span]
            seen = same & (ahead >= 0) & (ahead < LOOKBACK_SPAN)
            bias[t] = jnp.where(seen, 0.0, HIDDEN)

    def rows_of(block_refs, start, stop):
        pieces = []
        for b, ref in enumerate(block_refs):
            lo, hi = max(start, b * rows), min(stop, (b + 1) * rows)
            if lo < hi:
                pieces.append(ref[lo - b * rows : hi - b * rows, :])
        return jnp.concatenate(pieces, 0) if len(pieces) > 1 else pieces[0]

    for t in range(rows // tile):
        near = t * tile
        keys = rows_of(k_refs, near, near + span)
        values = rows_of(v_refs, near, near + span)
        for h in range(group):
            lanes = slice(h * HEAD_SIZE, (h + 1) * HEAD_SIZE)
            query = q_ref[near : near + tile, lanes]
            s = lax.dot_general(
                query, keys, (((1,), (1,)), ((), ())), preferred_element_type=jnp.float32
            )
            s = s + bias[t]
            top = jnp.max(s, axis=1, keepdims=True)
            w = jnp.exp2((s - top) * exp2_scale)
            total = jnp.sum(w, axis=1, keepdims=True)
            numer = jnp.dot(w.astype(jnp.bfloat16), values, preferred_element_type=jnp.float32)
            o_ref[near : near + tile, lanes] = (numer / total).astype(o_ref.dtype)


def attend(first, stride, query_states, keys, values, query_docs, key_docs):
    rows, width = query_states.shape
    kv_here = keys[0].shape[1] // HEAD_SIZE
    group = width // HEAD_SIZE // kv_here
    blocks = len(keys)
    heads = kv_here // stride
    tile = min(256, rows)
    wide = group * HEAD_SIZE
    span = LOOKBACK_SPAN + tile

    def head(i, first_ref):
        return (0, i * stride + first_ref[0])

    def whole(i, first_ref):
        return (0, 0)

    kv_spec = pl.BlockSpec((rows, HEAD_SIZE), head)
    return pl.pallas_call(
        functools.partial(attend_kernel, blocks, group, tile),
        out_shape=jax.ShapeDtypeStruct((rows, heads * wide), jnp.bfloat16),
        grid_spec=pltpu.PrefetchScalarGridSpec(
            num_scalar_prefetch=1,
            grid=(heads,),
            in_specs=[pl.BlockSpec((rows, wide), head)]
            + [kv_spec] * (2 * blocks)
            + [pl.BlockSpec((rows, 1), whole), pl.BlockSpec((1, blocks * rows), whole)],
            out_specs=pl.BlockSpec((rows, wide), lambda i, first_ref: (0, i)),
            scratch_shapes=[pltpu.VMEM((rows // tile, tile, span), jnp.float32)],
        ),
        compiler_params=pltpu.CompilerParams(vmem_limit_bytes=40 * 1024 * 1024),
        cost_estimate=pl.CostEstimate(
            flops=4 * heads * group * rows * span * HEAD_SIZE,
            bytes_accessed=2 * heads * rows * (2 * wide + 2 * blocks * HEAD_SIZE),
            transcendentals=heads * group * rows * span,
        ),
    )(first, query_states, *keys, *values, query_docs, key_docs)


def body(query_states, rotated_key_states, value_state_rows, doc_ids, w_out):
    tok_rows = query_states.shape[0]
    reach_count = LOOKBACK_SPAN // tok_rows
    shard_index = lax.axis_index("ctx")
    ctx, tp = lax.axis_size("ctx"), lax.axis_size("tp")
    kv_here = rotated_key_states.shape[1] // HEAD_SIZE
    columns = w_out.shape[1]
    half = -(-columns // 256) * 128
    paired = (
        ctx % 2 == 0
        and tp == 2
        and kv_here % 2 == 0
        and w_out.shape[0] * kv_here == query_states.shape[1]
        and columns % 128 == 0
    )
    parity = shard_index % 2

    docs, keys, values = [doc_ids], [rotated_key_states], [value_state_rows]
    for distance in range(1, reach_count + 1):
        got = shifted(doc_ids, "ctx", distance)
        docs.insert(0, jnp.where(shard_index >= distance, got, -1))
        keys.insert(0, shifted(rotated_key_states, "ctx", distance))
        values.insert(0, shifted(value_state_rows, "ctx", distance))
    query_docs = doc_ids[:, None]
    key_docs = jnp.concatenate(docs)[None, :]

    if not paired:
        all_w = lax.all_gather(w_out, "ctx", axis=0, tiled=True)
        first = jnp.zeros((1,), jnp.int32)
        attended = attend(first, 1, query_states, keys, values, query_docs, key_docs)
        all_heads = lax.all_gather(attended, "tp", axis=1, tiled=True)
        mixed = jnp.dot(all_heads, all_w, preferred_element_type=jnp.float32)
        return mixed.astype(jnp.bfloat16)

    shift = columns - half
    groups = [list(range(p, ctx, 2)) for p in range(2)]
    w_mine = lax.dynamic_slice_in_dim(w_out, parity * shift, half, 1)
    w_theirs = lax.dynamic_slice_in_dim(w_out, (1 - parity) * shift, half, 1)
    near_w = lax.all_gather(w_mine, "ctx", axis=0, tiled=True, axis_index_groups=groups)
    w_came = swapped(w_theirs, "ctx")
    far_w = lax.all_gather(w_came, "ctx", axis=0, tiled=True, axis_index_groups=groups)

    core = lax.axis_index("tp")

    def both_cores(part):
        other = swapped(part, "tp")
        low = jnp.where(core == 0, part, other)
        high = jnp.where(core == 0, other, part)
        return jnp.concatenate([low, high], 1)

    def heads_of(which):
        return attend(
            which.reshape(1).astype(jnp.int32), 2, query_states, keys, values, query_docs, key_docs
        )

    mine_near = heads_of(parity)
    theirs_far = swapped(mine_near, "ctx")
    mine_far = heads_of(1 - parity)
    theirs_near = swapped(mine_far, "ctx")

    def project(near, far):
        total = jnp.dot(both_cores(near), near_w, preferred_element_type=jnp.float32)
        total = total + jnp.dot(both_cores(far), far_w, preferred_element_type=jnp.float32)
        return total.astype(jnp.bfloat16)

    came = swapped(project(theirs_near, theirs_far), "ctx")
    made = project(mine_near, mine_far)
    left = jnp.where(parity == 0, made, came)
    right = jnp.where(parity == 0, came, made)
    return jnp.concatenate([left, right[:, 2 * half - columns :]], 1)


def solution(mesh):
    return jax.shard_map(
        body,
        mesh=mesh,
        in_specs=(P("ctx", "tp"), P("ctx", "tp"), P("ctx", "tp"), P("ctx"), P("ctx", "tp")),
        out_specs=P("ctx", "tp"),
        check_vma=False,
    )
```

```python
import functools
import jax
import jax.numpy as jnp
from jax import lax
from jax.experimental import pallas as pl
from jax.experimental.pallas import tpu as pltpu
from jax.sharding import PartitionSpec as P

HEAD_SIZE = 128
LOOKBACK_SPAN = 1024
HIDDEN = -1e30

attn_scale = 168.0 ** (-0.5)
exp2_scale = attn_scale * 1.4426950408889634


def shifted(value, axis, by):
    peers = lax.axis_size(axis)
    pairs = [(i, i + by) for i in range(peers) if 0 <= i + by < peers]
    return lax.ppermute(value, axis, pairs)


def swapped(value, axis):
    return lax.ppermute(value, axis, [(i, i ^ 1) for i in range(lax.axis_size(axis))])


def ring_gather(forward, backward):
    ctx = lax.axis_size("ctx")
    n = ctx // 2
    ring = list(range(0, n, 2)) + list(range(n - 1, 0, -2))
    place = lax.axis_index("ctx") // 2
    at = jnp.where(place % 2 == 0, place // 2, n - 1 - place // 2)
    rows, width = forward.shape
    held = [forward, backward]
    full = [jnp.zeros((n * rows, width), forward.dtype) for _ in held]
    for step in range(n):
        for way, sign in enumerate((1, -1)):
            if step:
                hops = [
                    (2 * ring[k] + p, 2 * ring[(k + sign) % n] + p)
                    for k in range(n)
                    for p in range(2)
                ]
                held[way] = lax.ppermute(held[way], "ctx", hops)
            k = (at - sign * step + n) % n
            origin = jnp.where(k < n // 2, 2 * k, 2 * (n - 1 - k) + 1)
            full[way] = lax.dynamic_update_slice_in_dim(full[way], held[way], origin * rows, 0)
    return full


def attend_kernel(blocks, group, tile, *refs):
    q_ref = refs[1]
    k_refs = refs[2 : 2 + blocks]
    v_refs = refs[2 + blocks : 2 + 2 * blocks]
    qdoc_ref, kdoc_ref, o_ref, bias = refs[2 + 2 * blocks :]
    rows = q_ref.shape[0]
    span = LOOKBACK_SPAN + tile

    @pl.when(pl.program_id(0) == 0)
    def _():
        for t in range(rows // tile):
            near = t * tile
            col = lax.broadcasted_iota(jnp.int32, (tile, span), 1)
            row = lax.broadcasted_iota(jnp.int32, (tile, span), 0)
            ahead = row + LOOKBACK_SPAN - col
            same = qdoc_ref[near : near + tile, :] == kdoc_ref[:, near : near + span]
            seen = same & (ahead >= 0) & (ahead < LOOKBACK_SPAN)
            bias[t] = jnp.where(seen, 0.0, HIDDEN)

    def rows_of(block_refs, start, stop):
        pieces = []
        for b, ref in enumerate(block_refs):
            lo, hi = max(start, b * rows), min(stop, (b + 1) * rows)
            if lo < hi:
                pieces.append(ref[lo - b * rows : hi - b * rows, :])
        return jnp.concatenate(pieces, 0) if len(pieces) > 1 else pieces[0]

    for t in range(rows // tile):
        near = t * tile
        keys = rows_of(k_refs, near, near + span)
        values = rows_of(v_refs, near, near + span)
        for h in range(group):
            lanes = slice(h * HEAD_SIZE, (h + 1) * HEAD_SIZE)
            query = q_ref[near : near + tile, lanes]
            s = lax.dot_general(
                query, keys, (((1,), (1,)), ((), ())), preferred_element_type=jnp.float32
            )
            s = s + bias[t]
            top = jnp.max(s, axis=1, keepdims=True)
            w = jnp.exp2((s - top) * exp2_scale)
            total = jnp.sum(w, axis=1, keepdims=True)
            numer = jnp.dot(w.astype(jnp.bfloat16), values, preferred_element_type=jnp.float32)
            o_ref[near : near + tile, lanes] = (numer / total).astype(o_ref.dtype)


def attend(first, stride, query_states, keys, values, query_docs, key_docs):
    rows, width = query_states.shape
    kv_here = keys[0].shape[1] // HEAD_SIZE
    group = width // HEAD_SIZE // kv_here
    blocks = len(keys)
    heads = kv_here // stride
    tile = min(256, rows)
    wide = group * HEAD_SIZE
    span = LOOKBACK_SPAN + tile

    def head(i, first_ref):
        return (0, i * stride + first_ref[0])

    def whole(i, first_ref):
        return (0, 0)

    kv_spec = pl.BlockSpec((rows, HEAD_SIZE), head)
    return pl.pallas_call(
        functools.partial(attend_kernel, blocks, group, tile),
        out_shape=jax.ShapeDtypeStruct((rows, heads * wide), jnp.bfloat16),
        grid_spec=pltpu.PrefetchScalarGridSpec(
            num_scalar_prefetch=1,
            grid=(heads,),
            in_specs=[pl.BlockSpec((rows, wide), head)]
            + [kv_spec] * (2 * blocks)
            + [pl.BlockSpec((rows, 1), whole), pl.BlockSpec((1, blocks * rows), whole)],
            out_specs=pl.BlockSpec((rows, wide), lambda i, first_ref: (0, i)),
            scratch_shapes=[pltpu.VMEM((rows // tile, tile, span), jnp.float32)],
        ),
        compiler_params=pltpu.CompilerParams(vmem_limit_bytes=40 * 1024 * 1024),
        cost_estimate=pl.CostEstimate(
            flops=4 * heads * group * rows * span * HEAD_SIZE,
            bytes_accessed=2 * heads * rows * (2 * wide + 2 * blocks * HEAD_SIZE),
            transcendentals=heads * group * rows * span,
        ),
    )(first, query_states, *keys, *values, query_docs, key_docs)


def body(query_states, rotated_key_states, value_state_rows, doc_ids, w_out):
    tok_rows = query_states.shape[0]
    reach_count = LOOKBACK_SPAN // tok_rows
    shard_index = lax.axis_index("ctx")
    ctx, tp = lax.axis_size("ctx"), lax.axis_size("tp")
    kv_here = rotated_key_states.shape[1] // HEAD_SIZE
    columns = w_out.shape[1]
    half = -(-columns // 256) * 128
    paired = (
        ctx % 4 == 0
        and tp == 2
        and kv_here % 2 == 0
        and w_out.shape[0] * kv_here == query_states.shape[1]
        and columns % 128 == 0
    )
    parity = shard_index % 2

    docs, keys, values = [doc_ids], [rotated_key_states], [value_state_rows]
    for distance in range(1, reach_count + 1):
        got = shifted(doc_ids, "ctx", distance)
        docs.insert(0, jnp.where(shard_index >= distance, got, -1))
        keys.insert(0, shifted(rotated_key_states, "ctx", distance))
        values.insert(0, shifted(value_state_rows, "ctx", distance))
    query_docs = doc_ids[:, None]
    key_docs = jnp.concatenate(docs)[None, :]

    if not paired:
        all_w = lax.all_gather(w_out, "ctx", axis=0, tiled=True)
        first = jnp.zeros((1,), jnp.int32)
        attended = attend(first, 1, query_states, keys, values, query_docs, key_docs)
        all_heads = lax.all_gather(attended, "tp", axis=1, tiled=True)
        mixed = jnp.dot(all_heads, all_w, preferred_element_type=jnp.float32)
        return mixed.astype(jnp.bfloat16)

    shift = columns - half
    w_mine = lax.dynamic_slice_in_dim(w_out, parity * shift, half, 1)
    w_theirs = lax.dynamic_slice_in_dim(w_out, (1 - parity) * shift, half, 1)
    near_w, far_w = ring_gather(w_mine, swapped(w_theirs, "ctx"))

    core = lax.axis_index("tp")

    def both_cores(part):
        other = swapped(part, "tp")
        low = jnp.where(core == 0, part, other)
        high = jnp.where(core == 0, other, part)
        return jnp.concatenate([low, high], 1)

    def heads_of(which):
        return attend(
            which.reshape(1).astype(jnp.int32), 2, query_states, keys, values, query_docs, key_docs
        )

    mine_near = heads_of(parity)
    theirs_far = swapped(mine_near, "ctx")
    mine_far = heads_of(1 - parity)
    theirs_near = swapped(mine_far, "ctx")

    def project(near, far):
        total = jnp.dot(both_cores(near), near_w, preferred_element_type=jnp.float32)
        total = total + jnp.dot(both_cores(far), far_w, preferred_element_type=jnp.float32)
        return total.astype(jnp.bfloat16)

    came = swapped(project(theirs_near, theirs_far), "ctx")
    made = project(mine_near, mine_far)
    left = jnp.where(parity == 0, made, came)
    right = jnp.where(parity == 0, came, made)
    return jnp.concatenate([left, right[:, 2 * half - columns :]], 1)


def solution(mesh):
    return jax.shard_map(
        body,
        mesh=mesh,
        in_specs=(P("ctx", "tp"), P("ctx", "tp"), P("ctx", "tp"), P("ctx"), P("ctx", "tp")),
        out_specs=P("ctx", "tp"),
        check_vma=False,
    )
```

```python
import functools
import jax
import jax.numpy as jnp
from jax import lax
from jax.experimental import pallas as pl
from jax.experimental.pallas import tpu as pltpu
from jax.sharding import PartitionSpec as P

HEAD_SIZE = 128
LOOKBACK_SPAN = 1024
HIDDEN = -1e30

attn_scale = 168.0 ** (-0.5)
exp2_scale = attn_scale * 1.4426950408889634


def shifted(value, axis, by):
    peers = lax.axis_size(axis)
    pairs = [(i, i + by) for i in range(peers) if 0 <= i + by < peers]
    return lax.ppermute(value, axis, pairs)


def swapped(value, axis):
    return lax.ppermute(value, axis, [(i, i ^ 1) for i in range(lax.axis_size(axis))])


def ring_gather(forward, backward):
    ctx = lax.axis_size("ctx")
    n = ctx // 2
    ring = list(range(0, n, 2)) + list(range(n - 1, 0, -2))
    place = lax.axis_index("ctx") // 2
    at = jnp.where(place % 2 == 0, place // 2, n - 1 - place // 2)
    rows, width = forward.shape
    held = [forward, backward]
    trail = []
    full = [jnp.zeros((n * rows, width), forward.dtype) for _ in held]
    for step in range(n):
        for way, sign in enumerate((1, -1)):
            if step:
                hops = [
                    (2 * ring[k] + p, 2 * ring[(k + sign) % n] + p)
                    for k in range(n)
                    for p in range(2)
                ]
                held[way] = lax.ppermute(held[way], "ctx", hops)
            k = (at - sign * step + n) % n
            origin = jnp.where(k < n // 2, 2 * k, 2 * (n - 1 - k) + 1)
            full[way] = lax.dynamic_update_slice_in_dim(full[way], held[way], origin * rows, 0)
        trail.append(list(held))
    return full, trail


def attend_kernel(blocks, group, tile, waits, *refs):
    q_ref = refs[1]
    k_refs = refs[2 : 2 + blocks]
    v_refs = refs[2 + blocks : 2 + 2 * blocks]
    qdoc_ref, kdoc_ref = refs[2 + 2 * blocks : 4 + 2 * blocks]
    o_ref, bias = refs[4 + 2 * blocks + waits :]
    rows = q_ref.shape[0]
    span = LOOKBACK_SPAN + tile

    @pl.when(pl.program_id(0) == 0)
    def _():
        for t in range(rows // tile):
            near = t * tile
            col = lax.broadcasted_iota(jnp.int32, (tile, span), 1)
            row = lax.broadcasted_iota(jnp.int32, (tile, span), 0)
            ahead = row + LOOKBACK_SPAN - col
            same = qdoc_ref[near : near + tile, :] == kdoc_ref[:, near : near + span]
            seen = same & (ahead >= 0) & (ahead < LOOKBACK_SPAN)
            bias[t] = jnp.where(seen, 0.0, HIDDEN)

    def rows_of(block_refs, start, stop):
        pieces = []
        for b, ref in enumerate(block_refs):
            lo, hi = max(start, b * rows), min(stop, (b + 1) * rows)
            if lo < hi:
                pieces.append(ref[lo - b * rows : hi - b * rows, :])
        return jnp.concatenate(pieces, 0) if len(pieces) > 1 else pieces[0]

    for t in range(rows // tile):
        near = t * tile
        keys = rows_of(k_refs, near, near + span)
        values = rows_of(v_refs, near, near + span)
        for h in range(group):
            lanes = slice(h * HEAD_SIZE, (h + 1) * HEAD_SIZE)
            query = q_ref[near : near + tile, lanes]
            s = lax.dot_general(
                query, keys, (((1,), (1,)), ((), ())), preferred_element_type=jnp.float32
            )
            s = s + bias[t]
            top = jnp.max(s, axis=1, keepdims=True)
            w = jnp.exp2((s - top) * exp2_scale)
            total = jnp.sum(w, axis=1, keepdims=True)
            numer = jnp.dot(w.astype(jnp.bfloat16), values, preferred_element_type=jnp.float32)
            o_ref[near : near + tile, lanes] = (numer / total).astype(o_ref.dtype)


def attend(first, stride, query_states, keys, values, query_docs, key_docs, after=()):
    rows, width = query_states.shape
    kv_here = keys[0].shape[1] // HEAD_SIZE
    group = width // HEAD_SIZE // kv_here
    blocks = len(keys)
    heads = kv_here // stride
    tile = min(256, rows)
    wide = group * HEAD_SIZE
    span = LOOKBACK_SPAN + tile

    def head(i, first_ref):
        return (0, i * stride + first_ref[0])

    def whole(i, first_ref):
        return (0, 0)

    kv_spec = pl.BlockSpec((rows, HEAD_SIZE), head)
    return pl.pallas_call(
        functools.partial(attend_kernel, blocks, group, tile, len(after)),
        out_shape=jax.ShapeDtypeStruct((rows, heads * wide), jnp.bfloat16),
        grid_spec=pltpu.PrefetchScalarGridSpec(
            num_scalar_prefetch=1,
            grid=(heads,),
            in_specs=[pl.BlockSpec((rows, wide), head)]
            + [kv_spec] * (2 * blocks)
            + [pl.BlockSpec((rows, 1), whole), pl.BlockSpec((1, blocks * rows), whole)]
            + [pl.BlockSpec(memory_space=pl.ANY)] * len(after),
            out_specs=pl.BlockSpec((rows, wide), lambda i, first_ref: (0, i)),
            scratch_shapes=[pltpu.VMEM((rows // tile, tile, span), jnp.float32)],
        ),
        compiler_params=pltpu.CompilerParams(vmem_limit_bytes=40 * 1024 * 1024),
        cost_estimate=pl.CostEstimate(
            flops=4 * heads * group * rows * span * HEAD_SIZE,
            bytes_accessed=2 * heads * rows * (2 * wide + 2 * blocks * HEAD_SIZE),
            transcendentals=heads * group * rows * span,
        ),
    )(first, query_states, *keys, *values, query_docs, key_docs, *after)


def body(query_states, rotated_key_states, value_state_rows, doc_ids, w_out):
    tok_rows = query_states.shape[0]
    reach_count = LOOKBACK_SPAN // tok_rows
    shard_index = lax.axis_index("ctx")
    ctx, tp = lax.axis_size("ctx"), lax.axis_size("tp")
    kv_here = rotated_key_states.shape[1] // HEAD_SIZE
    columns = w_out.shape[1]
    half = -(-columns // 256) * 128
    paired = (
        ctx % 4 == 0
        and tp == 2
        and kv_here % 2 == 0
        and w_out.shape[0] * kv_here == query_states.shape[1]
        and columns % 128 == 0
    )
    parity = shard_index % 2

    docs, keys, values = [doc_ids], [rotated_key_states], [value_state_rows]
    for distance in range(1, reach_count + 1):
        got = shifted(doc_ids, "ctx", distance)
        docs.insert(0, jnp.where(shard_index >= distance, got, -1))
        keys.insert(0, shifted(rotated_key_states, "ctx", distance))
        values.insert(0, shifted(value_state_rows, "ctx", distance))
    query_docs = doc_ids[:, None]
    key_docs = jnp.concatenate(docs)[None, :]

    if not paired:
        all_w = lax.all_gather(w_out, "ctx", axis=0, tiled=True)
        first = jnp.zeros((1,), jnp.int32)
        attended = attend(first, 1, query_states, keys, values, query_docs, key_docs)
        all_heads = lax.all_gather(attended, "tp", axis=1, tiled=True)
        mixed = jnp.dot(all_heads, all_w, preferred_element_type=jnp.float32)
        return mixed.astype(jnp.bfloat16)

    shift = columns - half
    w_mine = lax.dynamic_slice_in_dim(w_out, parity * shift, half, 1)
    w_theirs = lax.dynamic_slice_in_dim(w_out, (1 - parity) * shift, half, 1)
    (near_w, far_w), trail = ring_gather(w_mine, swapped(w_theirs, "ctx"))

    core = lax.axis_index("tp")

    def both_cores(part):
        other = swapped(part, "tp")
        low = jnp.where(core == 0, part, other)
        high = jnp.where(core == 0, other, part)
        return jnp.concatenate([low, high], 1)

    def heads_of(which, after):
        first = which.reshape(1).astype(jnp.int32)
        return attend(first, 2, query_states, keys, values, query_docs, key_docs, after)

    mine_near = heads_of(parity, trail[min(3, len(trail) - 1)])
    theirs_far = swapped(mine_near, "ctx")
    mine_far = heads_of(1 - parity, trail[min(4, len(trail) - 1)])
    theirs_near = swapped(mine_far, "ctx")

    def project(near, far):
        total = jnp.dot(both_cores(near), near_w, preferred_element_type=jnp.float32)
        total = total + jnp.dot(both_cores(far), far_w, preferred_element_type=jnp.float32)
        return total.astype(jnp.bfloat16)

    came = swapped(project(theirs_near, theirs_far), "ctx")
    made = project(mine_near, mine_far)
    left = jnp.where(parity == 0, made, came)
    right = jnp.where(parity == 0, came, made)
    return jnp.concatenate([left, right[:, 2 * half - columns :]], 1)


def solution(mesh):
    return jax.shard_map(
        body,
        mesh=mesh,
        in_specs=(P("ctx", "tp"), P("ctx", "tp"), P("ctx", "tp"), P("ctx"), P("ctx", "tp")),
        out_specs=P("ctx", "tp"),
        check_vma=False,
    )
```
